32 devices in a mesh: rep: 4 (over y, core), fsdp: 8 (over z, x).
Axes of the slice: x: 2, y: 2, z: 4, core: 2. Of those that a mesh axis runs over, the one named last changes fastest.
Arguments:
- codes: int32 [4, 4194304], P('rep', 'fsdp'), may hold values from 0 to 15
- scales: float32 [4, 65536], P('rep', 'fsdp'), may hold values from 0.02 to 0.3
- base: float32 [4194304], P('fsdp'), may hold values from -6 to 6
- momentum: float32 [4194304], P('fsdp'), may hold values from -3 to 3
- inputs: bfloat16 [4, 1024, 8192], P('rep', 'fsdp'), may hold values from -30 to 30
- gain: bfloat16 [4, 8192], P('rep', 'fsdp'), may hold values from 0.099609375 to 1.8984375
- cotangent: bfloat16 [4, 1024, 512], P('rep', 'fsdp'), may hold values from -0.5 to 0.5
Outputs:
- new_base: float32 [4194304], P('fsdp')
- new_momentum: float32 [4194304], P('fsdp')
- keys: bfloat16 [4, 1024, 512], P('rep', 'fsdp')
- grad_weight: float32 [4, 8192, 512], P('rep', 'fsdp')
- grad_gain: float32 [4, 8192], P('rep', 'fsdp')
The draws below stay inside these ranges and needn't reach their ends.
Inputs may be any that keep to these rules, and one draw needn't show every extreme that they name: `codes`: each entry is one 4-bit code.
All inputs are finite; a program needn't handle non-finite values.
Results may differ from the reference program's by a relative error of at most 0.015.
Values may be sent and summed in bfloat16 or wider, within the bound.
No kernel may reach another device: no remote copies, remote signals or barrier semaphores. Data moves between devices by JAX's collectives and lax.ppermute only.
A program may use at most 64 MiB of HBM per device.

```python
import math
import jax
import jax.numpy as jnp
from jax import lax

D = 8192
KV = 512
TOKENS_REP = 1024
F = 4194304
BLOCK = 64
N_REP = 4
N_FSDP = 8


def draw_inputs(key, part):
    key = jax.random.fold_in(key, 11)
    first, second, third = jax.random.split(key, 3)
    shape = (N_REP, TOKENS_REP, D)
    row_scale = jnp.exp(jax.random.uniform(first, (N_REP, TOKENS_REP, 1), jnp.float32, math.log(0.3), math.log(3.0)))
    col_scale = jnp.exp(jax.random.uniform(second, (1, 1, D), jnp.float32, math.log(0.3), math.log(3.0)))
    values = jax.random.normal(third, shape, jnp.float32)
    return jnp.clip(values * row_scale * col_scale, -30.0, 30.0).astype(jnp.bfloat16)


def touch_ends(drawn, stream_key, least, top_value):
    extent = drawn.shape
    index_at = [jax.random.randint(jax.random.fold_in(stream_key, axis), (), 0, extent[axis]) for axis in range(len(extent))]
    drawn = drawn.at[tuple(index_at)].set(least)
    longest = extent.index(max(extent))
    index_at[longest] = (index_at[longest] + 1) % extent[longest]
    return drawn.at[tuple(index_at)].set(top_value)


def levels(stream_key, dims, pieces, least, top_value):
    def one(position, blocks):
        draws = jax.random.uniform(jax.random.fold_in(jax.random.fold_in(stream_key, 6), position), (blocks,), jnp.float32, least / len(pieces), top_value / len(pieces))
        return jnp.repeat(jnp.exp(draws), dims[position] // blocks).reshape((-1,) + (1,) * (len(dims) - position - 1))

    loudness = one(*pieces[0])
    for cut in pieces[1:]:
        loudness = loudness * one(*cut)
    return loudness


def scatter_about(rng, dims, deviation, most, cuts=(), held_as=jnp.bfloat16):
    loudness = levels(rng, dims, cuts, -0.22, 0.18) if cuts else 1.0
    drawn = jax.random.normal(rng, dims, jnp.float32) * deviation * loudness
    return jnp.minimum(jnp.maximum(drawn, -most), most).astype(held_as)


def setup_inputs(seed: int = 0) -> dict:
    key_of = jax.random.split(jax.random.key(seed), 8)
    codes = touch_ends(jax.random.randint(key_of[0], (N_REP, F), 0, 16), jax.random.fold_in(key_of[0], 1), 0, 15).astype(jnp.int32)
    scales = jnp.clip(jnp.exp(math.log(0.3) - 2.7080503 * jax.random.uniform(key_of[1], (N_REP, F // BLOCK), jnp.float32) ** levels(key_of[1], (N_REP, F // BLOCK), ((0, 4), (1, 8)), -0.2, 0.2)), 0.02, 0.3)
    base = scatter_about(key_of[2], (F,), 1.0, 6.0, ((0, 8),), jnp.float32)
    momentum = scatter_about(key_of[3], (F,), 0.5, 3.0, ((0, 8),), jnp.float32)
    inputs = draw_inputs(jax.random.fold_in(key_of[7], 71), 0)
    gain = jnp.clip(1.0 + 0.18 * jax.random.normal(key_of[5], (N_REP, D), jnp.float32), 0.099609375, 1.8984375).astype(jnp.bfloat16)
    cotangent = scatter_about(key_of[6], (N_REP, TOKENS_REP, KV), (TOKENS_REP ** -0.5), 0.5, ((0, 4), (1, 8)))
    return {"codes": codes, "scales": scales, "base": base, "momentum": momentum, "inputs": inputs, "gain": gain, "cotangent": cotangent}


outer_rate = 0.7
momentum_decay = 0.9

def reference(codes, scales, base, momentum, inputs, gain, cotangent):
    decoded = (codes - 8).astype(jnp.float32) * jnp.repeat(scales, BLOCK, axis=1)
    average = lax.optimization_barrier(jnp.sum(decoded, axis=0)) / N_REP
    new_momentum = momentum_decay * momentum + average
    new_base = base - outer_rate * (average + momentum_decay * new_momentum)
    projection = (new_base.reshape(D, KV) * D ** (-0.5)).astype(jnp.bfloat16)
    group_rows = D // N_FSDP

    def one_replica(items):
        values, gains, upstream = items
        wide = values.astype(jnp.float32)
        inv_rms = lax.rsqrt(lax.optimization_barrier(jnp.mean(wide * wide, axis=1, keepdims=True)) + 1e-05)
        normed = (wide * inv_rms * gains.astype(jnp.float32)).astype(jnp.bfloat16)

        def add_group(total, group):
            start = group * group_rows
            cols = lax.dynamic_slice_in_dim(normed, start, group_rows, 1)
            rows = lax.dynamic_slice_in_dim(projection, start, group_rows, 0)
            part = jnp.dot(cols, rows, preferred_element_type=jnp.float32)
            part = lax.optimization_barrier(part.astype(jnp.bfloat16)).astype(jnp.float32)
            return (total + part, None)
        start_total = jnp.zeros((TOKENS_REP, KV), jnp.float32)
        key_total, unused = lax.scan(add_group, start_total, jnp.arange(N_FSDP, dtype=jnp.int32))
        grad_w = jnp.dot(normed.T, upstream, preferred_element_type=jnp.float32)
        back = jnp.dot(upstream, projection.T, preferred_element_type=jnp.float32)
        grad_g = lax.optimization_barrier(jnp.sum(back * wide * inv_rms, axis=0))
        return (key_total.astype(jnp.bfloat16), grad_w, grad_g)
    keys, grad_weight, grad_gain = lax.map(one_replica, (inputs, gain, cotangent))
    return (new_base, new_momentum, keys, grad_weight, grad_gain)
```

```python
import functools

import jax
import jax.numpy as jnp
from jax import lax
from jax.experimental import pallas as pl
from jax.experimental.pallas import tpu as pltpu
from jax.sharding import PartitionSpec as P

D = 8192
BLOCK = 64
LANES = 128
RIDER = 2
VMEM_LIMIT = 32 * 1024 * 1024


outer_rate = 0.7
momentum_decay = 0.9


def swap(value, axis, bit):
    return lax.ppermute(value, axis, [(i, i ^ bit) for i in range(lax.axis_size(axis))])


def params():
    return pltpu.CompilerParams(vmem_limit_bytes=VMEM_LIMIT)


def pack(block, width):
    tokens, key_width = block.shape
    if width >= key_width:
        rows = tokens * key_width // width
        return jnp.concatenate([block[at : at + rows] for at in range(0, tokens, rows)], axis=1)
    return jnp.concatenate([block[:, c : c + width] for c in range(0, key_width, width)], axis=0)


def unpack(rows, tokens, key_width):
    width = rows.shape[1]
    if width >= key_width:
        return jnp.concatenate([rows[:, c : c + key_width] for c in range(0, width, key_width)], axis=0)
    return jnp.concatenate([rows[at : at + tokens] for at in range(0, rows.shape[0], tokens)], axis=1)


def scale_kernel(me_ref, x_ref, near_ref, *far_refs):
    rows, features = x_ref.shape
    near, _, width = near_ref.shape
    step = 16
    first = me_ref[0] & ~(near - 1)

    @pl.loop(0, rows // step)
    def _(i):
        here = pl.ds(pl.multiple_of(i * step, step), step)
        total = jnp.zeros((step, LANES), jnp.float32)
        for c in range(0, features, LANES):
            part = x_ref[here, c : c + LANES].astype(jnp.float32)
            total = total + part * part
        mean = jnp.sum(total, axis=1, keepdims=True) * (1.0 / features)
        inv_rms = lax.rsqrt(mean + 1e-05)
        for at in range(near + len(far_refs)):
            owner = first + at if at < near else me_ref[0] ^ at
            start = pl.multiple_of(owner * width, width)
            part = x_ref[here, pl.ds(start, width)].astype(jnp.float32)
            part = (part * inv_rms).astype(jnp.bfloat16)
            if at < near:
                near_ref[at, here, :] = part
            else:
                far_refs[at - near][here, :] = part


def scale_inputs(activations, me, owners, above):
    tokens, features = activations.shape
    width = features // owners
    far = owners // 2
    rows = 32
    skips = [above if at == RIDER else 0 for at in range(far)]
    return pl.pallas_call(
        scale_kernel,
        grid_spec=pltpu.PrefetchScalarGridSpec(
            num_scalar_prefetch=1,
            grid=(tokens // rows,),
            in_specs=[pl.BlockSpec((rows, features), lambda i, me: (i, 0))],
            out_specs=[pl.BlockSpec((far, rows, width), lambda i, me: (0, i, 0))]
            + [pl.BlockSpec((rows, width), lambda i, me, skip=skip: (i + skip // rows, 0)) for skip in skips],
        ),
        out_shape=[jax.ShapeDtypeStruct((far, tokens, width), jnp.bfloat16)]
        + [jax.ShapeDtypeStruct((tokens + skip, width), jnp.bfloat16) for skip in skips],
        compiler_params=params(),
        cost_estimate=pl.CostEstimate(
            flops=4 * tokens * features, bytes_accessed=4 * tokens * features, transcendentals=tokens
        ),
        name="scale_inputs",
    )(me, activations)


def decode_kernel(half_ref, codes_ref, scales_ref, out_ref):
    group_rows = BLOCK
    row = lax.broadcasted_iota(jnp.int32, (group_rows, LANES), 0)
    lane = lax.broadcasted_iota(jnp.int32, (group_rows, LANES), 1)
    per_row = LANES // BLOCK
    own = lane // per_row == row
    k = lax.broadcasted_iota(jnp.int32, (2 * LANES, LANES), 0)
    n = lax.broadcasted_iota(jnp.int32, (2 * LANES, LANES), 1)
    spread = (k % per_row == n // BLOCK).astype(jnp.float32).astype(jnp.bfloat16)
    pieces = []
    for group in range(scales_ref.shape[0]):
        wide = jnp.broadcast_to(scales_ref[group : group + 1, :], (group_rows, LANES))
        wide = jnp.where(own, wide, 0.0)
        high = wide.astype(jnp.bfloat16)
        low = (wide - high.astype(jnp.float32)).astype(jnp.bfloat16)
        pieces.append(jnp.concatenate([high, low], axis=1))
    scale = jnp.dot(jnp.concatenate(pieces, axis=0), spread, preferred_element_type=jnp.float32)
    out_ref[...] = ((codes_ref[...] - 8).astype(jnp.float32) * scale).astype(jnp.bfloat16)


def decode(codes, scales, half):
    rows = codes.shape[0] // 2
    groups = scales.shape[0] // 2
    step = min(8, groups)
    steps = groups // step
    return pl.pallas_call(
        decode_kernel,
        grid_spec=pltpu.PrefetchScalarGridSpec(
            num_scalar_prefetch=1,
            grid=(steps,),
            in_specs=[
                pl.BlockSpec((rows // steps, LANES), lambda i, half: (half[0] * steps + i, 0)),
                pl.BlockSpec((step, LANES), lambda i, half: (half[0] * steps + i, 0)),
            ],
            out_specs=pl.BlockSpec((rows // steps, LANES), lambda i, half: (i, 0)),
        ),
        out_shape=jax.ShapeDtypeStruct((rows, LANES), jnp.bfloat16),
        compiler_params=params(),
        cost_estimate=pl.CostEstimate(flops=2 * rows * LANES, bytes_accessed=6 * rows * LANES, transcendentals=0),
        name="decode",
    )(half, codes, scales)


def update_kernel(replicas, core_ref, mine_ref, other_ref, base_ref, momentum_ref, base_out, momentum_out, weight_ref):
    own = pl.program_id(0) == core_ref[0]
    total = jnp.where(own, mine_ref[...].astype(jnp.float32), other_ref[...].astype(jnp.float32))
    average = total * (1.0 / replicas)
    new_momentum = momentum_decay * momentum_ref[...] + average
    momentum_out[...] = new_momentum
    base_out[...] = base_ref[...] - outer_rate * (average + momentum_decay * new_momentum)
    rows, width = weight_ref.shape
    cuts = width // LANES
    for c in range(cuts):
        part = base_out[pl.ds(c, rows, cuts), :]
        weight_ref[:, c * LANES : (c + 1) * LANES] = (part * D ** (-0.5)).astype(jnp.bfloat16)


def update(mine, other, core, base, momentum, replicas, key_width):
    rows = mine.shape[0]
    steps = 2
    weight_rows = 2 * rows * LANES // key_width
    half = pl.BlockSpec((rows // steps, LANES), lambda h, i, core: (i, 0))
    whole = pl.BlockSpec((rows // steps, LANES), lambda h, i, core: (h * steps + i, 0))
    full = jax.ShapeDtypeStruct((2 * rows, LANES), jnp.float32)
    return pl.pallas_call(
        functools.partial(update_kernel, replicas),
        grid_spec=pltpu.PrefetchScalarGridSpec(
            num_scalar_prefetch=1,
            grid=(2, steps),
            in_specs=[half, half, whole, whole],
            out_specs=[
                whole,
                whole,
                pl.BlockSpec((weight_rows // 2 // steps, key_width), lambda h, i, core: (h * steps + i, 0)),
            ],
        ),
        out_shape=[full, full, jax.ShapeDtypeStruct((weight_rows, key_width), jnp.bfloat16)],
        compiler_params=params(),
        cost_estimate=pl.CostEstimate(flops=12 * rows * LANES, bytes_accessed=40 * rows * LANES, transcendentals=0),
        name="update",
    )(core, mine, other, base, momentum)


def store_cuts(out_refs, orders, slot, part):
    cut = part.shape[1] // len(out_refs)
    for at, (out_ref, order) in enumerate(zip(out_refs, orders)):
        out_ref[order.index(slot)] = part[:, at * cut : (at + 1) * cut]


def near_keys_kernel(orders, me_ref, x_ref, weight_ref, gain_ref, *out_refs):
    gain = gain_ref[...].astype(jnp.float32)
    weight = weight_ref[...]
    near, tokens, _ = out_refs[0].shape
    for slot in range(near):
        x = x_ref[(me_ref[0] & (near - 1)) ^ slot, x_ref.shape[1] - tokens :, :]
        normed = (x.astype(jnp.float32) * gain).astype(jnp.bfloat16)
        part = jnp.dot(normed, weight, preferred_element_type=jnp.float32).astype(jnp.bfloat16)
        store_cuts(out_refs, orders, slot, part)


def near_partial_keys(columns, me, tokens, orders, weight, gain):
    near, _, width = columns.shape
    key_width = weight.shape[1]
    flops = 2 * near * tokens * width * key_width
    whole = pl.BlockSpec(memory_space=pltpu.VMEM)
    cut = jax.ShapeDtypeStruct((near, tokens, key_width // len(orders)), jnp.bfloat16)
    return pl.pallas_call(
        functools.partial(near_keys_kernel, orders),
        in_specs=[pl.BlockSpec(memory_space=pltpu.SMEM), whole, whole, whole],
        out_specs=[whole] * len(orders),
        out_shape=[cut] * len(orders),
        compiler_params=params(),
        cost_estimate=pl.CostEstimate(flops=flops, bytes_accessed=flops // 256, transcendentals=0),
        name="near_partial_keys",
    )(me, columns, weight, gain)


def far_keys_kernel(orders, *refs):
    *x_refs, weight_ref, gain_ref = refs[: -len(orders)]
    out_refs = refs[-len(orders) :]
    gain = gain_ref[...].astype(jnp.float32)
    weight = weight_ref[...]
    tokens = out_refs[0].shape[1]
    for slot, x_ref in enumerate(x_refs):
        x = x_ref[x_ref.shape[0] - tokens :, :]
        normed = (x.astype(jnp.float32) * gain).astype(jnp.bfloat16)
        part = jnp.dot(normed, weight, preferred_element_type=jnp.float32).astype(jnp.bfloat16)
        store_cuts(out_refs, orders, slot, part)


def far_partial_keys(blocks, tokens, orders, weight, gain):
    width, key_width = weight.shape
    flops = 2 * len(blocks) * tokens * width * key_width
    cut = jax.ShapeDtypeStruct((len(blocks), tokens, key_width // len(orders)), jnp.bfloat16)
    return pl.pallas_call(
        functools.partial(far_keys_kernel, orders),
        out_shape=[cut] * len(orders),
        compiler_params=params(),
        cost_estimate=pl.CostEstimate(flops=flops, bytes_accessed=flops // 256, transcendentals=0),
        name="far_partial_keys",
    )(*blocks, weight, gain)


def by_bits(count, bits):
    return sorted(range(count), key=lambda slot: [bool(slot & bit) for bit in bits])


def fold(near, far, bits, spread):
    for bit in bits:
        middle = near.shape[0] // 2
        got = swap(jnp.concatenate([near[middle:], far[middle:], spread], axis=0), "fsdp", bit)
        near = add(near[:middle], got[:middle])
        far = add(far[:middle], got[middle : 2 * middle])
        spread = jnp.concatenate([spread, got[2 * middle :]], axis=0)
    return near[0], far[0], spread


def spread_slots(bits):
    slots = [0]
    for bit in bits:
        slots = slots + [slot ^ bit for slot in slots]
    return slots


def add(*parts):
    return sum(part.astype(jnp.float32) for part in parts).astype(jnp.bfloat16)


def grads_kernel(orders, me_ref, x_ref, gain_ref, weight_ref, *refs):
    *others, rows_ref, total_ref = refs
    far_refs, token_refs = others[: -len(orders)], others[-len(orders) :]
    near, rows, _ = x_ref.shape
    tokens, key_width = token_refs[0].shape[1], weight_ref.shape[1]
    i = pl.program_id(0)
    cut = rows_ref.shape[0]
    columns = pl.ds(pl.multiple_of(i * cut, cut), cut)
    blocks, upstream = [], []
    for slot in range(near):
        at = (me_ref[0] & (near - 1)) ^ slot
        far_ref = far_refs[slot ^ RIDER]
        blocks += [x_ref[at, rows - tokens :, columns], far_ref[far_ref.shape[0] - tokens :, :]]
        upstream += [
            unpack(x_ref[at, : rows - tokens, :], tokens, key_width),
            jnp.concatenate([ref[order.index(slot)] for ref, order in zip(token_refs, orders)], axis=1),
        ]
    x = jnp.concatenate(blocks, axis=0).astype(jnp.float32)
    upstream = jnp.concatenate(upstream, axis=0)
    normed = (x * gain_ref[...].astype(jnp.float32)).astype(jnp.bfloat16)
    rows_ref[...] = lax.dot_general(
        normed, upstream, (((0,), (0,)), ((), ())), preferred_element_type=jnp.float32
    )
    back = lax.dot_general(
        upstream, weight_ref[...], (((1,), (1,)), ((), ())), preferred_element_type=jnp.float32
    )
    total_ref[...] = jnp.sum(back * x, axis=0, keepdims=True)


def grads(columns, far_blocks, far_tokens, orders, me, gain, weight):
    near, _, width = columns.shape
    tokens, key_width = far_tokens[0].shape[1], weight.shape[1]
    cut = min(256, width)
    flops = 8 * near * tokens * width * key_width
    return pl.pallas_call(
        functools.partial(grads_kernel, orders),
        grid_spec=pltpu.PrefetchScalarGridSpec(
            num_scalar_prefetch=1,
            grid=(width // cut,),
            in_specs=[
                pl.BlockSpec(columns.shape, lambda i, me: (0, 0, 0)),
                pl.BlockSpec((1, cut), lambda i, me: (0, i)),
                pl.BlockSpec((cut, key_width), lambda i, me: (i, 0)),
            ]
            + [pl.BlockSpec((block.shape[0], cut), lambda i, me: (0, i)) for block in far_blocks]
            + [pl.BlockSpec(one.shape, lambda i, me: (0, 0, 0)) for one in far_tokens],
            out_specs=[
                pl.BlockSpec((cut, key_width), lambda i, me: (i, 0)),
                pl.BlockSpec((1, cut), lambda i, me: (0, i)),
            ],
        ),
        out_shape=[
            jax.ShapeDtypeStruct((width, key_width), jnp.float32),
            jax.ShapeDtypeStruct((1, width), jnp.float32),
        ],
        compiler_params=params(),
        cost_estimate=pl.CostEstimate(flops=flops, bytes_accessed=flops // 512, transcendentals=0),
        name="grads",
    )(me, columns, gain, weight, *far_blocks, *far_tokens)


def sum_over_replicas(codes, scales, core):
    give = decode(codes, scales, 1 - core)
    keep = decode(codes, scales, core)
    total = keep.astype(jnp.float32) + swap(give, "rep", 1).astype(jnp.float32)
    bit = 2
    while bit < lax.axis_size("rep"):
        mine = total.astype(jnp.bfloat16)
        total = mine.astype(jnp.float32) + swap(mine, "rep", bit).astype(jnp.float32)
        bit *= 2
    mine = total.astype(jnp.bfloat16)
    return mine, swap(mine, "rep", 1)


def stage(work, *operands):
    def nothing(*operands):
        made = jax.eval_shape(work, *operands)
        return tuple(jnp.zeros(one.shape, one.dtype) for one in made)

    return lax.cond(lax.axis_index("fsdp") < lax.axis_size("fsdp"), work, nothing, *operands)


def shards(codes, scales, base, momentum, inputs, gain, cotangent):
    activations = inputs[0]
    upstream = cotangent[0]
    tokens, key_width = upstream.shape
    owners = lax.axis_size("fsdp")
    replicas = lax.axis_size("rep")
    me = lax.axis_index("fsdp").astype(jnp.int32)[None]
    core = (lax.axis_index("rep").astype(jnp.int32) & 1)[None]
    far = owners // 2
    bits = [1 << k for k in range(far.bit_length() - 1)]

    width = activations.shape[1] // owners
    packed = pack(upstream, width)
    above = packed.shape[0]
    near, *scaled = scale_inputs(activations, me, owners, above)
    near, *scaled, codes = lax.optimization_barrier((near, *scaled, codes))
    scaled[RIDER] = scaled[RIDER].at[:above].set(packed)
    far_blocks = [swap(scaled[slot], "fsdp", far + slot) for slot in range(far)]

    halves = [[half * far + i for i in range(far)] for half in range(2)]
    swapped = [bits[1], bits[0]] + bits[2:]
    orders = [by_bits(far, each) for each in (bits, swapped)]

    def beside(codes, scales, base, momentum, near, packed, gain):
        near = jnp.concatenate([jnp.broadcast_to(packed, (far, *packed.shape)), near], axis=1)
        columns = lax.all_to_all(near, "fsdp", split_axis=0, concat_axis=0, tiled=True, axis_index_groups=halves)
        mine, other = sum_over_replicas(codes, scales, core)
        updated = update(mine, other, core, base, momentum, replicas, key_width)
        weight = updated[-1]
        return *updated, columns, *near_partial_keys(columns, me, tokens, orders, weight, gain)

    new_base, new_momentum, weight, columns, *near_parts = stage(
        beside,
        codes.reshape(-1, LANES),
        scales.reshape(-1, LANES),
        base.reshape(-1, LANES),
        momentum.reshape(-1, LANES),
        near,
        packed,
        gain,
    )

    rider = far_blocks[RIDER]
    far_tokens = jnp.split(unpack(rider[: rider.shape[0] - tokens], tokens, key_width)[None], 2, axis=2)
    far_parts = far_partial_keys(far_blocks, tokens, orders, weight, gain)
    folded = [fold(*each) for each in zip(near_parts, far_parts, (bits, swapped), far_tokens)]
    own, given, spread = zip(*folded)
    given, columns, *spread = lax.optimization_barrier((jnp.concatenate(given, axis=1), columns, *spread))
    keys = add(jnp.concatenate(own, axis=1), swap(given, "fsdp", far))

    slots = [spread_slots(bits), spread_slots(swapped)]
    grad_rows, grad_total = grads(columns, far_blocks, spread, slots, me, gain, weight)
    return (
        new_base.reshape(-1),
        new_momentum.reshape(-1),
        keys[None],
        grad_rows[None],
        grad_total,
    )


def solution(mesh):
    placed = (
        P("rep", "fsdp"),
        P("rep", "fsdp"),
        P("fsdp"),
        P("fsdp"),
        P("rep", "fsdp", None),
        P("rep", "fsdp"),
        P("rep", "fsdp", None),
    )
    return jax.shard_map(
        shards,
        mesh=mesh,
        in_specs=placed,
        out_specs=(
            P("fsdp"),
            P("fsdp"),
            P("rep", "fsdp", None),
            P("rep", "fsdp", None),
            P("rep", "fsdp"),
        ),
        check_vma=False,
    )
```

```python
import functools

import jax
import jax.numpy as jnp
from jax import lax
from jax.experimental import pallas as pl
from jax.experimental.pallas import tpu as pltpu
from jax.sharding import PartitionSpec as P

D = 8192
BLOCK = 64
LANES = 128
RIDER = 2
VMEM_LIMIT = 32 * 1024 * 1024


outer_rate = 0.7
momentum_decay = 0.9


def swap(value, axis, bit):
    return lax.ppermute(value, axis, [(i, i ^ bit) for i in range(lax.axis_size(axis))])


def params():
    return pltpu.CompilerParams(vmem_limit_bytes=VMEM_LIMIT)


def pack(block, width):
    tokens, key_width = block.shape
    if width >= key_width:
        rows = tokens * key_width // width
        return jnp.concatenate([block[at : at + rows] for at in range(0, tokens, rows)], axis=1)
    return jnp.concatenate([block[:, c : c + width] for c in range(0, key_width, width)], axis=0)


def unpack(rows, tokens, key_width):
    width = rows.shape[1]
    if width >= key_width:
        return jnp.concatenate([rows[:, c : c + key_width] for c in range(0, width, key_width)], axis=0)
    return jnp.concatenate([rows[at : at + tokens] for at in range(0, rows.shape[0], tokens)], axis=1)


def scale_kernel(me_ref, x_ref, near_ref, *far_refs):
    rows, features = x_ref.shape
    near, _, width = near_ref.shape
    step = 16
    first = me_ref[0] & ~(near - 1)

    @pl.loop(0, rows // step)
    def _(i):
        here = pl.ds(pl.multiple_of(i * step, step), step)
        total = jnp.zeros((step, LANES), jnp.float32)
        for c in range(0, features, LANES):
            part = x_ref[here, c : c + LANES].astype(jnp.float32)
            total = total + part * part
        mean = jnp.sum(total, axis=1, keepdims=True) * (1.0 / features)
        inv_rms = lax.rsqrt(mean + 1e-05)
        for at in range(near + len(far_refs)):
            owner = first + at if at < near else me_ref[0] ^ at
            start = pl.multiple_of(owner * width, width)
            part = x_ref[here, pl.ds(start, width)].astype(jnp.float32)
            part = (part * inv_rms).astype(jnp.bfloat16)
            if at < near:
                near_ref[at, here, :] = part
            else:
                far_refs[at - near][here, :] = part


def scale_inputs(activations, me, owners, above):
    tokens, features = activations.shape
    width = features // owners
    far = owners // 2
    rows = 32
    skips = [above if at == RIDER else 0 for at in range(far)]
    return pl.pallas_call(
        scale_kernel,
        grid_spec=pltpu.PrefetchScalarGridSpec(
            num_scalar_prefetch=1,
            grid=(tokens // rows,),
            in_specs=[pl.BlockSpec((rows, features), lambda i, me: (i, 0))],
            out_specs=[pl.BlockSpec((far, rows, width), lambda i, me: (0, i, 0))]
            + [pl.BlockSpec((rows, width), lambda i, me, skip=skip: (i + skip // rows, 0)) for skip in skips],
        ),
        out_shape=[jax.ShapeDtypeStruct((far, tokens, width), jnp.bfloat16)]
        + [jax.ShapeDtypeStruct((tokens + skip, width), jnp.bfloat16) for skip in skips],
        compiler_params=params(),
        cost_estimate=pl.CostEstimate(
            flops=4 * tokens * features, bytes_accessed=4 * tokens * features, transcendentals=tokens
        ),
        name="scale_inputs",
    )(me, activations)


def decode_kernel(half_ref, codes_ref, scales_ref, out_ref):
    group_rows = BLOCK
    row = lax.broadcasted_iota(jnp.int32, (group_rows, LANES), 0)
    lane = lax.broadcasted_iota(jnp.int32, (group_rows, LANES), 1)
    per_row = LANES // BLOCK
    own = lane // per_row == row
    k = lax.broadcasted_iota(jnp.int32, (2 * LANES, LANES), 0)
    n = lax.broadcasted_iota(jnp.int32, (2 * LANES, LANES), 1)
    spread = (k % per_row == n // BLOCK).astype(jnp.float32).astype(jnp.bfloat16)
    pieces = []
    for group in range(scales_ref.shape[0]):
        wide = jnp.broadcast_to(scales_ref[group : group + 1, :], (group_rows, LANES))
        wide = jnp.where(own, wide, 0.0)
        high = wide.astype(jnp.bfloat16)
        low = (wide - high.astype(jnp.float32)).astype(jnp.bfloat16)
        pieces.append(jnp.concatenate([high, low], axis=1))
    scale = jnp.dot(jnp.concatenate(pieces, axis=0), spread, preferred_element_type=jnp.float32)
    out_ref[...] = ((codes_ref[...] - 8).astype(jnp.float32) * scale).astype(jnp.bfloat16)


def decode(codes, scales, half):
    rows = codes.shape[0] // 2
    groups = scales.shape[0] // 2
    step = min(8, groups)
    steps = groups // step
    return pl.pallas_call(
        decode_kernel,
        grid_spec=pltpu.PrefetchScalarGridSpec(
            num_scalar_prefetch=1,
            grid=(steps,),
            in_specs=[
                pl.BlockSpec((rows // steps, LANES), lambda i, half: (half[0] * steps + i, 0)),
                pl.BlockSpec((step, LANES), lambda i, half: (half[0] * steps + i, 0)),
            ],
            out_specs=pl.BlockSpec((rows // steps, LANES), lambda i, half: (i, 0)),
        ),
        out_shape=jax.ShapeDtypeStruct((rows, LANES), jnp.bfloat16),
        compiler_params=params(),
        cost_estimate=pl.CostEstimate(flops=2 * rows * LANES, bytes_accessed=6 * rows * LANES, transcendentals=0),
        name="decode",
    )(half, codes, scales)


def update_kernel(replicas, core_ref, mine_ref, other_ref, base_ref, momentum_ref, base_out, momentum_out, weight_ref):
    own = pl.program_id(0) == core_ref[0]
    total = jnp.where(own, mine_ref[...].astype(jnp.float32), other_ref[...].astype(jnp.float32))
    average = total * (1.0 / replicas)
    new_momentum = momentum_decay * momentum_ref[...] + average
    momentum_out[...] = new_momentum
    base_out[...] = base_ref[...] - outer_rate * (average + momentum_decay * new_momentum)
    rows, width = weight_ref.shape
    cuts = width // LANES
    for c in range(cuts):
        part = base_out[pl.ds(c, rows, cuts), :]
        weight_ref[:, c * LANES : (c + 1) * LANES] = (part * D ** (-0.5)).astype(jnp.bfloat16)


def update(mine, other, core, base, momentum, replicas, key_width):
    rows = mine.shape[0]
    steps = 2
    weight_rows = 2 * rows * LANES // key_width
    half = pl.BlockSpec((rows // steps, LANES), lambda h, i, core: (i, 0))
    whole = pl.BlockSpec((rows // steps, LANES), lambda h, i, core: (h * steps + i, 0))
    full = jax.ShapeDtypeStruct((2 * rows, LANES), jnp.float32)
    return pl.pallas_call(
        functools.partial(update_kernel, replicas),
        grid_spec=pltpu.PrefetchScalarGridSpec(
            num_scalar_prefetch=1,
            grid=(2, steps),
            in_specs=[half, half, whole, whole],
            out_specs=[
                whole,
                whole,
                pl.BlockSpec((weight_rows // 2 // steps, key_width), lambda h, i, core: (h * steps + i, 0)),
            ],
        ),
        out_shape=[full, full, jax.ShapeDtypeStruct((weight_rows, key_width), jnp.bfloat16)],
        compiler_params=params(),
        cost_estimate=pl.CostEstimate(flops=12 * rows * LANES, bytes_accessed=40 * rows * LANES, transcendentals=0),
        name="update",
    )(core, mine, other, base, momentum)


def store_cuts(out_refs, orders, slot, part):
    cut = part.shape[1] // len(out_refs)
    for at, (out_ref, order) in enumerate(zip(out_refs, orders)):
        out_ref[order.index(slot)] = part[:, at * cut : (at + 1) * cut]


def keys_kernel(orders, me_ref, columns_ref, *refs):
    cuts = len(orders)
    *x_refs, weight_ref, gain_ref = refs[: -2 * cuts]
    near_refs, far_refs = refs[-2 * cuts : -cuts], refs[-cuts:]
    gain = gain_ref[...].astype(jnp.float32)
    weight = weight_ref[...]
    near, tokens, _ = near_refs[0].shape
    for out_refs in (far_refs, near_refs):
        for slot in range(near):
            if out_refs is far_refs:
                x = x_refs[slot][x_refs[slot].shape[0] - tokens :, :]
            else:
                x = columns_ref[(me_ref[0] & (near - 1)) ^ slot, columns_ref.shape[1] - tokens :, :]
            normed = (x.astype(jnp.float32) * gain).astype(jnp.bfloat16)
            part = jnp.dot(normed, weight, preferred_element_type=jnp.float32).astype(jnp.bfloat16)
            store_cuts(out_refs, orders, slot, part)


def partial_keys(columns, blocks, me, tokens, orders, weight, gain):
    width, key_width = weight.shape
    near = len(blocks)
    flops = 4 * near * tokens * width * key_width
    whole = pl.BlockSpec(memory_space=pltpu.VMEM)
    cut = jax.ShapeDtypeStruct((near, tokens, key_width // len(orders)), jnp.bfloat16)
    parts = pl.pallas_call(
        functools.partial(keys_kernel, orders),
        in_specs=[pl.BlockSpec(memory_space=pltpu.SMEM)] + [whole] * (near + 3),
        out_specs=[whole] * (2 * len(orders)),
        out_shape=[cut] * (2 * len(orders)),
        compiler_params=params(),
        cost_estimate=pl.CostEstimate(flops=flops, bytes_accessed=flops // 256, transcendentals=0),
        name="partial_keys",
    )(me, columns, *blocks, weight, gain)
    return parts[: len(orders)], parts[len(orders) :]


def by_bits(count, bits):
    return sorted(range(count), key=lambda slot: [bool(slot & bit) for bit in bits])


def fold(near, far, bits, spread):
    for bit in bits:
        middle = near.shape[0] // 2
        got = swap(jnp.concatenate([near[middle:], far[middle:], spread], axis=0), "fsdp", bit)
        near = add(near[:middle], got[:middle])
        far = add(far[:middle], got[middle : 2 * middle])
        spread = jnp.concatenate([spread, got[2 * middle :]], axis=0)
    return near[0], far[0], spread


def spread_slots(bits):
    slots = [0]
    for bit in bits:
        slots = slots + [slot ^ bit for slot in slots]
    return slots


def add(*parts):
    return sum(part.astype(jnp.float32) for part in parts).astype(jnp.bfloat16)


def grads_kernel(orders, me_ref, x_ref, gain_ref, weight_ref, *refs):
    *others, rows_ref, total_ref = refs
    far_refs, token_refs = others[: -len(orders)], others[-len(orders) :]
    near, rows, _ = x_ref.shape
    tokens, key_width = token_refs[0].shape[1], weight_ref.shape[1]
    i = pl.program_id(0)
    cut = rows_ref.shape[0]
    columns = pl.ds(pl.multiple_of(i * cut, cut), cut)
    blocks, upstream = [], []
    for slot in range(near):
        at = (me_ref[0] & (near - 1)) ^ slot
        far_ref = far_refs[slot ^ RIDER]
        blocks += [x_ref[at, rows - tokens :, columns], far_ref[far_ref.shape[0] - tokens :, :]]
        upstream += [
            unpack(x_ref[at, : rows - tokens, :], tokens, key_width),
            jnp.concatenate([ref[order.index(slot)] for ref, order in zip(token_refs, orders)], axis=1),
        ]
    x = jnp.concatenate(blocks, axis=0).astype(jnp.float32)
    upstream = jnp.concatenate(upstream, axis=0)
    normed = (x * gain_ref[...].astype(jnp.float32)).astype(jnp.bfloat16)
    rows_ref[...] = lax.dot_general(
        normed, upstream, (((0,), (0,)), ((), ())), preferred_element_type=jnp.float32
    )
    back = lax.dot_general(
        upstream, weight_ref[...], (((1,), (1,)), ((), ())), preferred_element_type=jnp.float32
    )
    total_ref[...] = jnp.sum(back * x, axis=0, keepdims=True)


def grads(columns, far_blocks, far_tokens, orders, me, gain, weight):
    near, _, width = columns.shape
    tokens, key_width = far_tokens[0].shape[1], weight.shape[1]
    cut = min(256, width)
    flops = 8 * near * tokens * width * key_width
    return pl.pallas_call(
        functools.partial(grads_kernel, orders),
        grid_spec=pltpu.PrefetchScalarGridSpec(
            num_scalar_prefetch=1,
            grid=(width // cut,),
            in_specs=[
                pl.BlockSpec(columns.shape, lambda i, me: (0, 0, 0)),
                pl.BlockSpec((1, cut), lambda i, me: (0, i)),
                pl.BlockSpec((cut, key_width), lambda i, me: (i, 0)),
            ]
            + [pl.BlockSpec((block.shape[0], cut), lambda i, me: (0, i)) for block in far_blocks]
            + [pl.BlockSpec(one.shape, lambda i, me: (0, 0, 0)) for one in far_tokens],
            out_specs=[
                pl.BlockSpec((cut, key_width), lambda i, me: (i, 0)),
                pl.BlockSpec((1, cut), lambda i, me: (0, i)),
            ],
        ),
        out_shape=[
            jax.ShapeDtypeStruct((width, key_width), jnp.float32),
            jax.ShapeDtypeStruct((1, width), jnp.float32),
        ],
        compiler_params=params(),
        cost_estimate=pl.CostEstimate(flops=flops, bytes_accessed=flops // 512, transcendentals=0),
        name="grads",
    )(me, columns, gain, weight, *far_blocks, *far_tokens)


def sum_over_replicas(codes, scales, core):
    give = decode(codes, scales, 1 - core)
    keep = decode(codes, scales, core)
    total = keep.astype(jnp.float32) + swap(give, "rep", 1).astype(jnp.float32)
    bit = 2
    while bit < lax.axis_size("rep"):
        mine = total.astype(jnp.bfloat16)
        total = mine.astype(jnp.float32) + swap(mine, "rep", bit).astype(jnp.float32)
        bit *= 2
    mine = total.astype(jnp.bfloat16)
    return mine, swap(mine, "rep", 1)


def stage(work, *operands):
    def nothing(*operands):
        made = jax.eval_shape(work, *operands)
        return tuple(jnp.zeros(one.shape, one.dtype) for one in made)

    return lax.cond(lax.axis_index("fsdp") < lax.axis_size("fsdp"), work, nothing, *operands)


def shards(codes, scales, base, momentum, inputs, gain, cotangent):
    activations = inputs[0]
    upstream = cotangent[0]
    tokens, key_width = upstream.shape
    owners = lax.axis_size("fsdp")
    replicas = lax.axis_size("rep")
    me = lax.axis_index("fsdp").astype(jnp.int32)[None]
    core = (lax.axis_index("rep").astype(jnp.int32) & 1)[None]
    far = owners // 2
    bits = [1 << k for k in range(far.bit_length() - 1)]

    width = activations.shape[1] // owners
    packed = pack(upstream, width)
    above = packed.shape[0]
    near, *scaled = scale_inputs(activations, me, owners, above)
    near, *scaled, codes = lax.optimization_barrier((near, *scaled, codes))
    scaled[RIDER] = scaled[RIDER].at[:above].set(packed)
    far_blocks = [swap(scaled[slot], "fsdp", far + slot) for slot in range(far)]

    halves = [[half * far + i for i in range(far)] for half in range(2)]
    swapped = [bits[1], bits[0]] + bits[2:]
    orders = [by_bits(far, each) for each in (bits, swapped)]

    def beside(codes, scales, base, momentum, near, packed):
        near = jnp.concatenate([jnp.broadcast_to(packed, (far, *packed.shape)), near], axis=1)
        columns = lax.all_to_all(near, "fsdp", split_axis=0, concat_axis=0, tiled=True, axis_index_groups=halves)
        mine, other = sum_over_replicas(codes, scales, core)
        updated = update(mine, other, core, base, momentum, replicas, key_width)
        return *updated, columns

    new_base, new_momentum, weight, columns = stage(
        beside,
        codes.reshape(-1, LANES),
        scales.reshape(-1, LANES),
        base.reshape(-1, LANES),
        momentum.reshape(-1, LANES),
        near,
        packed,
    )

    rider = far_blocks[RIDER]
    far_tokens = jnp.split(unpack(rider[: rider.shape[0] - tokens], tokens, key_width)[None], 2, axis=2)
    near_parts, far_parts = partial_keys(columns, far_blocks, me, tokens, orders, weight, gain)
    folded = [fold(*each) for each in zip(near_parts, far_parts, (bits, swapped), far_tokens)]
    own, given, spread = zip(*folded)
    given, columns, *spread = lax.optimization_barrier((jnp.concatenate(given, axis=1), columns, *spread))
    keys = add(jnp.concatenate(own, axis=1), swap(given, "fsdp", far))

    slots = [spread_slots(bits), spread_slots(swapped)]
    grad_rows, grad_total = grads(columns, far_blocks, spread, slots, me, gain, weight)
    return (
        new_base.reshape(-1),
        new_momentum.reshape(-1),
        keys[None],
        grad_rows[None],
        grad_total,
    )


def solution(mesh):
    placed = (
        P("rep", "fsdp"),
        P("rep", "fsdp"),
        P("fsdp"),
        P("fsdp"),
        P("rep", "fsdp", None),
        P("rep", "fsdp"),
        P("rep", "fsdp", None),
    )
    return jax.shard_map(
        shards,
        mesh=mesh,
        in_specs=placed,
        out_specs=(
            P("fsdp"),
            P("fsdp"),
            P("rep", "fsdp", None),
            P("rep", "fsdp", None),
            P("rep", "fsdp"),
        ),
        check_vma=False,
    )
```
